128 devices in a mesh: tsnk: 8 (over y, z_hi), tsrc: 16 (over x, z_lo, core).
Axes of the slice: x: 4, y: 4, z: 4 (z_hi: 2, z_lo: 2; z = z_hi * 2 + z_lo), core: 2. Of those that a mesh axis runs over, the one named last changes fastest.
Arguments:
- perambulator: bfloat16 [16, 16, 2, 384, 384], P('tsnk', 'tsrc'), may hold values from -0.5 to 0.5
- elementals: bfloat16 [16, 2, 2, 384, 384], P('tsrc'), may hold values from -0.5 to 0.5
- op_mom: int32 [4, 2], replicated, may hold values from 0 to 1
Outputs:
- correlators: float32 [16, 16, 3, 2, 4, 4], P('tsnk', 'tsrc')
The draws below stay inside these ranges and needn't reach their ends.
All inputs are finite; a program needn't handle non-finite values.
Results may differ from the reference program's by a relative error of at most 0.0067.
Values may be sent and summed in bfloat16 or wider, within the bound.
A program may use at most 128 MiB of HBM per device.

```python
import jax
import jax.numpy as jnp
from jax import lax

NV = 384
NMOM = 2
NOPS = 4
TIMES = 16


def set_ends(drawn, own_key, least, largest):
    dims = drawn.shape
    place = [jax.random.randint(jax.random.fold_in(own_key, axis), (), 0, dims[axis]) for axis in range(len(dims))]
    drawn = drawn.at[tuple(place)].set(least)
    longest = dims.index(max(dims))
    place[longest] = (place[longest] + 1) % dims[longest]
    return drawn.at[tuple(place)].set(largest)


def block_scale(own_key, shape, split, low, largest):
    loudness, own = 1.0, jax.random.fold_in(own_key, 6)
    for position, shards_of in split:
        steps = jnp.exp(jax.random.uniform(jax.random.fold_in(own, position), (shards_of,), jnp.float32, low / len(split), largest / len(split)))
        loudness = loudness * jnp.repeat(steps, shape[position] // shards_of).reshape([-1 if axis == position else 1 for axis in range(len(shape))])
    return loudness


def scatter_about(stream_key, extent, deviation, bound, cuts=(), kind=jnp.bfloat16):
    level = block_scale(stream_key, extent, cuts, -0.22, 0.18) if cuts else 1.0
    values = jax.random.normal(stream_key, extent, jnp.float32) * deviation * level
    return jnp.minimum(jnp.maximum(values, -bound), bound).astype(kind)


def setup_inputs(seed: int = 0) -> dict:
    keys = jax.random.split(jax.random.key(seed), 4)
    return {
        "perambulator": scatter_about(keys[0], (TIMES, TIMES, 2, NV, NV), ((2 * NV) ** -0.5), 0.5, ((0, 8), (1, 16))),
        "elementals": scatter_about(keys[1], (TIMES, NMOM, 2, NV, NV), ((2 * NV) ** -0.5), 0.5, ((0, 16),)),
        "op_mom": set_ends(jax.random.randint(keys[2], (NOPS, 2), 0, NMOM), jax.random.fold_in(keys[2], 1), 0, NMOM - 1).astype(jnp.int32),
    }


def cmul(left, right):
    real_part = jnp.dot(left[0], right[0], preferred_element_type=jnp.float32) - jnp.dot(left[1], right[1], preferred_element_type=jnp.float32)
    imag_part = jnp.dot(left[0], right[1], preferred_element_type=jnp.float32) + jnp.dot(left[1], right[0], preferred_element_type=jnp.float32)
    return jnp.stack([real_part, imag_part]).astype(jnp.bfloat16)


def dagger(block):
    return jnp.stack([block[0].T, -block[1].T])


def trace_table(first, second):
    count = first.shape[0]
    other = second.shape[0]
    width = first.shape[-1] * first.shape[-1]
    flat_a = first.reshape(count, 2, width)
    flat_b = jnp.swapaxes(second, -1, -2).reshape(other, 2, width)
    def inner(u, v):
        return lax.dot_general(flat_a[:, u], flat_b[:, v], (((1,), (1,)), ((), ())), preferred_element_type=jnp.float32)
    real_part = inner(0, 0) - inner(1, 1)
    imag_part = inner(0, 1) + inner(1, 0)
    return jnp.stack([real_part, imag_part])


def pair_correlators(forward, sink_el, source_el, diag_snk, diag_src, op_mom):
    moms = sink_el.shape[0]
    backward = dagger(forward)
    q_list = [cmul(source_el[m], backward) for m in range(moms)]
    x_list = [cmul(forward, q_list[m]) for m in range(moms)]
    g_list = [cmul(forward, source_el[m]) for m in range(moms)]
    r_list = [cmul(diag_src, q_list[m]) for m in range(moms)]
    s_list = [cmul(sink_el[m], diag_snk) for m in range(moms)]
    l_arr = jnp.stack([cmul(sink_el[a], g_list[m]) for a in range(moms) for m in range(moms)])
    p_arr = jnp.stack([cmul(sink_el[a], x_list[m]) for a in range(moms) for m in range(moms)])
    m_arr = jnp.stack([cmul(r_list[m], s_list[a]) for m in range(moms) for a in range(moms)])
    box = trace_table(p_arr, p_arr).reshape(2, moms, moms, moms, moms)
    rect = trace_table(l_arr, m_arr).reshape(2, moms, moms, moms, moms)
    tri = trace_table(l_arr, jnp.stack(r_list)).reshape(2, moms, moms, moms)
    one_a = op_mom[:, 0][:, None]
    two_a = op_mom[:, 1][:, None]
    one_b = op_mom[:, 0][None, :]
    two_b = op_mom[:, 1][None, :]
    box_out = box[:, one_a, one_b, two_a, two_b]
    rect_out = rect[:, one_a, one_b, two_b, two_a]
    tri_out = tri[:, one_a, one_b, two_b]
    return jnp.stack([box_out, rect_out, tri_out])


def reference(perambulator, elementals, op_mom):
    count = perambulator.shape[0]
    def one_pair(index):
        sink = index // count
        source = index % count
        forward = perambulator[sink, source]
        return pair_correlators(forward, elementals[sink], elementals[source], perambulator[sink, sink], perambulator[source, source], op_mom)
    table = lax.map(one_pair, jnp.arange(count * count, dtype=jnp.int32))
    return table.reshape((count, count) + table.shape[1:])
```

```python
import jax
import jax.numpy as jnp
from jax import lax
from jax.experimental import pallas as pl
from jax.experimental.pallas import tpu as pltpu
from jax.sharding import PartitionSpec as P

N = 384
W = 2 * N
BF = jnp.bfloat16
NN = (((1,), (0,)), ((), ()))
NT = (((1,), (1,)), ((), ()))
MESH = pl.DeviceIdType.MESH


def wait_for(ref, sem):
    pltpu.make_async_copy(ref, ref, sem).wait()


class Gather:
    def __init__(self, buf, place, device, send_sem, recv_sem):
        self.buf, self.send_sem, self.recv_sem = buf, send_sem, recv_sem
        a, b = place // 2, place % 2
        self.other = device(a * 2 + 1 - b)
        self.right = device(lax.rem(a + 1, 4) * 2 + b)
        self.left = device(lax.rem(a + 3, 4) * 2 + b)
        self.a, self.b = a, b
        self.sent = []

    def slot(self, step, flip):
        b = 1 - self.b if flip else self.b
        return lax.rem(self.a + step, 4) * 2 + b

    def send(self, slot, to):
        n = len(self.sent)
        copy = pltpu.make_async_remote_copy(
            src_ref=self.buf.at[slot], dst_ref=self.buf.at[slot], send_sem=self.send_sem.at[n],
            recv_sem=self.recv_sem.at[slot], device_id=to, device_id_type=MESH)
        copy.start()
        self.sent.append(copy)

    def wait(self, slot):
        wait_for(self.buf.at[slot], self.recv_sem.at[slot])

    def own(self):
        mine = self.slot(0, False)
        self.wait(mine)
        for to in (self.other, self.right, self.left):
            self.send(mine, to)

    def pair(self):
        slot = self.slot(0, True)
        self.wait(slot)
        for to in (self.right, self.left):
            self.send(slot, to)

    def sides(self):
        for step in (3, 1):
            for flip in (False, True):
                self.wait(self.slot(step, flip))
        self.send(self.slot(3, False), self.right)
        self.send(self.slot(1, True), self.left)

    def last(self):
        for flip in (False, True):
            self.wait(self.slot(2, flip))

    def drain(self):
        for copy in self.sent:
            copy.wait_send()


def rows(r, i):
    return jnp.concatenate([r, i], axis=1)


def block(r, i):
    return jnp.concatenate([rows(r, i), rows(-i, r)], axis=0)


def block_t(r, i):
    return jnp.concatenate([rows(r, -i), rows(i, r)], axis=0)


def mul(left, right, dims=NN):
    return lax.dot_general(left, right, dims, preferred_element_type=jnp.float32).astype(BF)


def exact(left, right):
    return lax.dot_general(
        left, right, NN, precision=lax.Precision.HIGHEST, preferred_element_type=jnp.float32)


def halves(ref):
    return ref[:, :N], ref[:, N:]


def parts(ref):
    count, depth = ref.shape[0] // 2, ref.shape[1]
    return ref[:count].reshape(count * depth, N), ref[count:].reshape(count * depth, N)


def elemental(ref, m):
    return parts(ref.at[pl.ds(4 * m, 4)])


def two(ref, s):
    return jnp.concatenate([ref[s, 0], ref[s, 1]], axis=0)


def forward_products(f, psi, g):
    def body(b, _):
        left = jnp.concatenate([rows(*parts(f.at[s])) for s in range(2)], axis=0)
        out = mul(left, block(*elemental(psi, b)))
        g[0, b] = out[:N]
        g[1, b] = out[N:]
        return 0
    lax.fori_loop(0, 2, body, 0)


def back_products(f, psi, q):
    def body(s, _):
        left = jnp.concatenate([rows(*elemental(psi, b)) for b in range(2)], axis=0)
        out = mul(left, block(*parts(f.at[s])), NT)
        q[s, 0] = out[:N]
        q[s, 1] = out[N:]
        return 0
    lax.fori_loop(0, 2, body, 0)


def from_left(left, s, q, out):
    def body(b, _):
        out[s, b] = mul(rows(*parts(left)), block(*halves(q.at[s, b])))
        return 0
    lax.fori_loop(0, 2, body, 0)


def loop_products(s, g, r, y):
    def body(b, _):
        out = mul(two(g, s), block(*halves(r.at[s, b])))
        y[s, b] = out[:N]
        y[s, 2 + b] = out[N:]
        return 0
    lax.fori_loop(0, 2, body, 0)


def box_products(s, phi, x, p, pt):
    def body(b, _):
        left = jnp.concatenate([rows(*elemental(phi.at[s], a)) for a in range(2)], axis=0)
        out = mul(left, block(*halves(x.at[s, b])))
        for a in range(2):
            part = out[a * N:(a + 1) * N]
            p[s, 2 * a + b] = part
            pt[s, 2 * a + b] = rows(part[:, :N].T, part[:, N:].T)
        return 0
    lax.fori_loop(0, 2, body, 0)


def sink_transposes(s, phi, phit):
    def body(a, _):
        r, i = elemental(phi.at[s], a)
        phit[s, a] = rows(r.T, i.T)
        return 0
    lax.fori_loop(0, 2, body, 0)


def sink_products(s, phi, phit, df, st, zt):
    left = jnp.concatenate([rows(*elemental(phi.at[s], a)) for a in range(2)], axis=0)
    out = mul(left, block(*parts(df)))
    st[0] = out[:N]
    st[1] = out[N:]

    def second(a, _):
        out = mul(two(phit, s), block_t(*halves(st.at[a])), NT)
        zt[s, 2 * a] = out[:N]
        zt[s, 2 * a + 1] = out[N:]
        return 0
    lax.fori_loop(0, 2, second, 0)


def grouped(refs):
    out = []
    for ref in refs:
        for c in range(2):
            out.append(jnp.concatenate(
                [ref[32 * k:32 * k + 32, c * N:(c + 1) * N] for k in range(N // 32)], axis=1))
    return jnp.concatenate(out, axis=0)


def iotas(shape):
    return lax.broadcasted_iota(jnp.int32, shape, 0), lax.broadcasted_iota(jnp.int32, shape, 1)


def diagonal(left, right):
    acc = lax.dot_general(grouped(left), grouped(right), NT, preferred_element_type=jnp.float32)
    r, c = iotas(acc.shape)
    kept = jnp.where(r % 32 == c % 32, acc, 0.0)
    return jnp.sum(kept.reshape(acc.shape[0] // 32, 32, acc.shape[1]), axis=1)


def chosen(op, which, index):
    out = jnp.zeros(index.shape, jnp.int32)
    for p in range(4):
        out = jnp.where(index == p, op[which, p], out)
    return out


def as_f32(mask):
    return jnp.where(mask, 1.0, 0.0).astype(jnp.float32)


def put(out, s, k, table):
    out[s, 0, k, 0] = table[0:4, 0:4] - table[4:8, 4:8]
    out[s, 0, k, 1] = table[0:4, 4:8] + table[4:8, 0:4]


def box_traces(s, op, p, pt, out):
    acc = diagonal([p.at[s, k] for k in range(4)], [pt.at[s, k] for k in range(4)])
    r, c = iotas((16, 8))
    pick = (r // 8 == (c // 2) % 2) & ((r // 4) % 2 == c % 2) & (chosen(op, 0, r % 4) == c // 4)
    half = exact(as_f32(pick), acc)
    r, c = iotas((256, 16))
    pick = (r // 128 == c // 8) & ((r // 32) % 2 == (c // 4) % 2) & (chosen(op, 1, c % 4) == (r // 64) % 2)
    full = exact(half, as_f32(pick))
    r, c = iotas((16, 16))
    keep = (chosen(op, 0, c % 4) == r // 8) & (chosen(op, 1, r % 4) == c // 8)
    full = jnp.where(keep, full, 0.0)
    full = full[0:8] + full[8:16]
    put(out, s, 0, full[:, 0:8] + full[:, 8:16])


def loop_traces(s, op, zt, phit, y, out):
    acc = diagonal(
        [zt.at[s, k] for k in range(4)] + [phit.at[s, a] for a in range(2)], [y.at[s, k] for k in range(4)])
    acc = jnp.concatenate([acc, jnp.zeros((4, 256), jnp.float32)], axis=0)
    r, c = iotas((256, 8))
    pick = ((r // 32) % 2 == c // 4) & (chosen(op, 0, c % 4) == r // 128) & (chosen(op, 1, c % 4) == (r // 64) % 2)
    half = exact(acc, as_f32(pick))
    r, c = iotas((16, 16))
    rect = (r < 8) & (c < 8) & (c // 4 == chosen(op, 1, r % 4)) & ((c // 2) % 2 == chosen(op, 0, r % 4))
    tri = (r >= 8) & (c >= 8) & ((c - 8) // 2 == chosen(op, 0, r % 4))
    pick = (rect | tri) & ((r // 4) % 2 == c % 2)
    full = exact(as_f32(pick), half)
    put(out, s, 1, full[0:8])
    put(out, s, 2, full[8:16])


def kernel(op, f, psi, out, phi, df, di, g, x, q, r, y, p, pt, phit, st, zt,
           phi_send, phi_recv, df_send, df_recv, di_send, di_recv, swap_send, root_send,
           twin_send, twin_recv, z_send, z_recv):
    j = lax.axis_index("tsnk")
    column = lax.axis_index("tsrc")
    k, c = column // 2, column % 2
    twin = 1 - c
    swapped = (k, 2 * j + c)
    sibling = (j, 2 * k + twin)

    def in_row(q):
        return (j, 2 * q + c)

    def in_column(q):
        return (q, 2 * k + c)

    phi_ring = Gather(phi.at[c], k, in_row, phi_send, phi_recv)
    df_ring = Gather(df, k, in_row, df_send, df_recv)
    di_ring = Gather(di, j, in_column, di_send, di_recv)

    barrier = pltpu.get_barrier_semaphore()

    def greet(to):
        pl.semaphore_signal(barrier, inc=1, device_id=to, device_id_type=MESH)

    for to in (sibling, di_ring.other, di_ring.right, di_ring.left, phi_ring.other, phi_ring.right, phi_ring.left):
        greet(to)

    def mates(do):
        for q in range(8):
            @pl.when(q != j)
            def _():
                do(q)

    @pl.when(j == k)
    def _():
        def both(q):
            greet(in_row(q))
            greet(in_column(q))
        mates(both)
        pl.semaphore_wait(barrier, 21)

    @pl.when(j != k)
    def _():
        greet(swapped)
        greet((j, 2 * j + c))
        greet((k, 2 * k + c))
        pl.semaphore_wait(barrier, 10)

    def scatter(q, buf, sems, n, to):
        return pltpu.make_async_remote_copy(
            src_ref=f.at[c, q], dst_ref=buf.at[q], send_sem=root_send.at[8 * n + q], recv_sem=sems.at[q],
            device_id=to, device_id_type=MESH)

    def swap():
        return pltpu.make_async_remote_copy(
            src_ref=psi.at[j], dst_ref=phi.at[c, j], send_sem=swap_send, recv_sem=phi_recv.at[j],
            device_id=swapped, device_id_type=MESH)

    @pl.when(j == k)
    def _():
        pltpu.make_async_copy(f.at[c, j], di.at[j], di_recv.at[j]).start()
        mates(lambda q: scatter(q, di, di_recv, 0, in_column(q)).start())
        pltpu.make_async_copy(psi.at[j], phi.at[c, j], phi_recv.at[j]).start()
        pltpu.make_async_copy(f.at[c, j], df.at[j], df_recv.at[j]).start()
        mates(lambda q: scatter(q, df, df_recv, 1, in_row(q)).start())

    @pl.when(j != k)
    def _():
        swap().start()

    to_twin = []

    def share(step):
        a = lax.rem(k // 2 + step, 4)
        piece = phi.at[c, pl.ds(2 * a, 2)]
        copy = pltpu.make_async_remote_copy(
            src_ref=piece, dst_ref=piece, send_sem=twin_send.at[a], recv_sem=twin_recv.at[a],
            device_id=sibling, device_id_type=MESH)
        copy.start()
        to_twin.append(copy)

    forward_products(f, psi, g)
    di_ring.own()
    back_products(f, psi, q)
    di_ring.pair()
    phi_ring.own()
    from_left(f.at[0], 0, q, x)
    di_ring.sides()
    phi_ring.pair()
    share(0)
    from_left(f.at[1], 1, q, x)
    di_ring.last()
    from_left(di, 0, q, r)
    phi_ring.sides()
    share(3)
    share(1)
    from_left(di, 1, q, r)
    df_ring.own()
    phi_ring.last()
    share(2)
    loop_products(0, g, r, y)
    df_ring.pair()
    loop_products(1, g, r, y)
    df_ring.sides()
    box_products(c, phi, x, p, pt)
    sink_transposes(c, phi, phit)
    df_ring.last()
    sink_products(c, phi, phit, df, st, zt)
    z_copy = pltpu.make_async_remote_copy(
        src_ref=zt.at[c], dst_ref=zt.at[c], send_sem=z_send, recv_sem=z_recv, device_id=sibling, device_id_type=MESH)
    z_copy.start()
    box_traces(c, op, p, pt, out)
    for a in range(4):
        wait_for(phi.at[twin, pl.ds(2 * a, 2)], twin_recv.at[a])
    box_products(twin, phi, x, p, pt)
    sink_transposes(twin, phi, phit)
    box_traces(twin, op, p, pt, out)
    loop_traces(c, op, zt, phit, y, out)
    wait_for(zt.at[twin], z_recv)
    loop_traces(twin, op, zt, phit, y, out)

    for ring in (di_ring, phi_ring, df_ring):
        ring.drain()
    for copy in to_twin + [z_copy]:
        copy.wait_send()

    @pl.when(j == k)
    def _():
        mates(lambda q: scatter(q, di, di_recv, 0, in_column(q)).wait_send())
        mates(lambda q: scatter(q, df, df_recv, 1, in_row(q)).wait_send())

    @pl.when(j != k)
    def _():
        swap().wait_send()


def on_device(perambulator, elementals, op_mom):
    f = perambulator.reshape(2, 8, 2 * N // 8, N)
    psi = elementals.reshape(8, 4 * N // 8, N)
    vmem = pl.BlockSpec(memory_space=pltpu.VMEM)
    sems = pltpu.SemaphoreType.DMA
    return pl.pallas_call(
        kernel,
        out_shape=jax.ShapeDtypeStruct((2, 1, 3, 2, 4, 4), jnp.float32),
        in_specs=[pl.BlockSpec(memory_space=pltpu.SMEM), vmem, vmem],
        out_specs=vmem,
        scratch_shapes=[
            pltpu.VMEM((2, 8, 4 * N // 8, N), BF),
            pltpu.VMEM((8, 2 * N // 8, N), BF),
            pltpu.VMEM((8, 2 * N // 8, N), BF),
            pltpu.VMEM((2, 2, N, W), BF),
            pltpu.VMEM((2, 2, N, W), BF),
            pltpu.VMEM((2, 2, N, W), BF),
            pltpu.VMEM((2, 2, N, W), BF),
            pltpu.VMEM((2, 4, N, W), BF),
            pltpu.VMEM((2, 4, N, W), BF),
            pltpu.VMEM((2, 4, N, W), BF),
            pltpu.VMEM((2, 2, N, W), BF),
            pltpu.VMEM((2, N, W), BF),
            pltpu.VMEM((2, 4, N, W), BF),
            sems((7,)), sems((8,)), sems((7,)), sems((8,)), sems((7,)), sems((8,)),
            sems, sems((16,)), sems((4,)), sems((4,)), sems, sems,
        ],
        compiler_params=pltpu.CompilerParams(
            collective_id=0, has_side_effects=True, vmem_limit_bytes=60 * 2**20),
        cost_estimate=pl.CostEstimate(flops=20_000_000_000, bytes_accessed=4_000_000, transcendentals=0),
    )(op_mom.T, f, psi)


def solution(mesh):
    placed = (P("tsnk", "tsrc", None, None, None), P("tsrc", None, None, None, None), P())
    return jax.shard_map(
        on_device,
        mesh=mesh,
        in_specs=placed,
        out_specs=P("tsnk", "tsrc", None, None, None, None),
        check_vma=False,
    )
```

```python
import jax
import jax.numpy as jnp
from jax import lax
from jax.experimental import pallas as pl
from jax.experimental.pallas import tpu as pltpu
from jax.sharding import PartitionSpec as P

N = 384
W = 2 * N
BF = jnp.bfloat16
NN = (((1,), (0,)), ((), ()))
NT = (((1,), (1,)), ((), ()))
MESH = pl.DeviceIdType.MESH


def wait_for(ref, sem):
    pltpu.make_async_copy(ref, ref, sem).wait()


def rows(r, i):
    return jnp.concatenate([r, i], axis=1)


def block(r, i):
    return jnp.concatenate([rows(r, i), rows(-i, r)], axis=0)


def block_t(r, i):
    return jnp.concatenate([rows(r, -i), rows(i, r)], axis=0)


def mul(left, right, dims=NN):
    return lax.dot_general(left, right, dims, preferred_element_type=jnp.float32).astype(BF)


def exact(left, right):
    return lax.dot_general(
        left, right, NN, precision=lax.Precision.HIGHEST, preferred_element_type=jnp.float32)


def halves(ref):
    return ref[:, :N], ref[:, N:]


def parts(ref):
    count, depth = ref.shape[0] // 2, ref.shape[1]
    return ref[:count].reshape(count * depth, N), ref[count:].reshape(count * depth, N)


def two(ref, s):
    return jnp.concatenate([ref[s, 0], ref[s, 1]], axis=0)


def forward_products(f, psi, g):
    def body(b, _):
        left = jnp.concatenate([rows(*parts(f.at[s])) for s in range(2)], axis=0)
        out = mul(left, block(*parts(psi.at[b])))
        g[0, b] = out[:N]
        g[1, b] = out[N:]
        return 0
    lax.fori_loop(0, 2, body, 0)


def back_products(f, psi, q):
    def body(s, _):
        left = jnp.concatenate([rows(*parts(psi.at[b])) for b in range(2)], axis=0)
        out = mul(left, block(*parts(f.at[s])), NT)
        q[s, 0] = out[:N]
        q[s, 1] = out[N:]
        return 0
    lax.fori_loop(0, 2, body, 0)


def from_left(left, s, q, out):
    def body(b, _):
        out[s, b] = mul(rows(*parts(left)), block(*halves(q.at[s, b])))
        return 0
    lax.fori_loop(0, 2, body, 0)


def loop_products(s, g, r, y):
    def body(b, _):
        out = mul(two(g, s), block(*halves(r.at[s, b])))
        y[s, b] = out[:N]
        y[s, 2 + b] = out[N:]
        return 0
    lax.fori_loop(0, 2, body, 0)


def box_products(s, a, phi, x, p, pt):
    def body(b, _):
        out = mul(rows(*parts(phi.at[s, a])), block(*halves(x.at[s, b])))
        p[s, 2 * a + b] = out
        pt[s, 2 * a + b] = rows(out[:, :N].T, out[:, N:].T)
        return 0
    lax.fori_loop(0, 2, body, 0)


def sink_transposes(s, phi, phit):
    def body(a, _):
        r, i = parts(phi.at[s, a])
        phit[s, a] = rows(r.T, i.T)
        return 0
    lax.fori_loop(0, 2, body, 0)


def sink_products(s, phi, phit, df, st, zt):
    left = jnp.concatenate([rows(*parts(phi.at[s, a])) for a in range(2)], axis=0)
    out = mul(left, block(*parts(df)))
    st[0] = out[:N]
    st[1] = out[N:]

    def second(a, _):
        out = mul(two(phit, s), block_t(*halves(st.at[a])), NT)
        zt[s, 2 * a] = out[:N]
        zt[s, 2 * a + 1] = out[N:]
        return 0
    lax.fori_loop(0, 2, second, 0)


def grouped(refs):
    out = []
    for ref in refs:
        for c in range(2):
            out.append(jnp.concatenate(
                [ref[32 * k:32 * k + 32, c * N:(c + 1) * N] for k in range(N // 32)], axis=1))
    return jnp.concatenate(out, axis=0)


def iotas(shape):
    return lax.broadcasted_iota(jnp.int32, shape, 0), lax.broadcasted_iota(jnp.int32, shape, 1)


def diagonal(left, right):
    acc = lax.dot_general(grouped(left), grouped(right), NT, preferred_element_type=jnp.float32)
    r, c = iotas(acc.shape)
    kept = jnp.where(r % 32 == c % 32, acc, 0.0)
    return jnp.sum(kept.reshape(acc.shape[0] // 32, 32, acc.shape[1]), axis=1)


def chosen(op, which, index):
    out = jnp.zeros(index.shape, jnp.int32)
    for p in range(4):
        out = jnp.where(index == p, op[which, p], out)
    return out


def as_f32(mask):
    return jnp.where(mask, 1.0, 0.0).astype(jnp.float32)


def put(out, s, k, table):
    out[s, 0, k, 0] = table[0:4, 0:4] - table[4:8, 4:8]
    out[s, 0, k, 1] = table[0:4, 4:8] + table[4:8, 0:4]


def box_traces(s, op, p, pt, out):
    acc = diagonal([p.at[s, k] for k in range(4)], [pt.at[s, k] for k in range(4)])
    r, c = iotas((16, 8))
    pick = (r // 8 == (c // 2) % 2) & ((r // 4) % 2 == c % 2) & (chosen(op, 0, r % 4) == c // 4)
    half = exact(as_f32(pick), acc)
    r, c = iotas((256, 16))
    pick = (r // 128 == c // 8) & ((r // 32) % 2 == (c // 4) % 2) & (chosen(op, 1, c % 4) == (r // 64) % 2)
    full = exact(half, as_f32(pick))
    r, c = iotas((16, 16))
    keep = (chosen(op, 0, c % 4) == r // 8) & (chosen(op, 1, r % 4) == c // 8)
    full = jnp.where(keep, full, 0.0)
    full = full[0:8] + full[8:16]
    put(out, s, 0, full[:, 0:8] + full[:, 8:16])


def loop_traces(s, op, zt, phit, y, out):
    acc = diagonal(
        [zt.at[s, k] for k in range(4)] + [phit.at[s, a] for a in range(2)], [y.at[s, k] for k in range(4)])
    acc = jnp.concatenate([acc, jnp.zeros((4, 256), jnp.float32)], axis=0)
    r, c = iotas((256, 8))
    pick = ((r // 32) % 2 == c // 4) & (chosen(op, 0, c % 4) == r // 128) & (chosen(op, 1, c % 4) == (r // 64) % 2)
    half = exact(acc, as_f32(pick))
    r, c = iotas((16, 16))
    rect = (r < 8) & (c < 8) & (c // 4 == chosen(op, 1, r % 4)) & ((c // 2) % 2 == chosen(op, 0, r % 4))
    tri = (r >= 8) & (c >= 8) & ((c - 8) // 2 == chosen(op, 0, r % 4))
    pick = (rect | tri) & ((r // 4) % 2 == c % 2)
    full = exact(as_f32(pick), half)
    put(out, s, 1, full[0:8])
    put(out, s, 2, full[8:16])


def kernel(op, f_hbm, psi_hbm, out, f, psi, phi, df, di, g, x, q, r, y, p, pt, phit, st, zt,
           phi_send, phi_recv, df_send, df_recv, di_send, di_recv, root_send,
           twin_send, twin_recv, z_send, z_recv, load_sem):
    j = lax.axis_index("tsnk")
    column = lax.axis_index("tsrc")
    k, c = column // 2, column % 2
    twin = 1 - c
    sibling = (j, 2 * k + twin)

    def later(place, step):
        return lax.rem(place + step, 8)

    def remote(src, dst, send, recv, to):
        return pltpu.make_async_remote_copy(
            src_ref=src, dst_ref=dst, send_sem=send, recv_sem=recv, device_id=to, device_id_type=MESH)

    loads = [pltpu.make_async_copy(psi_hbm, psi, load_sem.at[0]), pltpu.make_async_copy(f_hbm, f, load_sem.at[1])]
    for copy in loads:
        copy.start()

    barrier = pltpu.get_barrier_semaphore()

    def greet(to):
        pl.semaphore_signal(barrier, inc=1, device_id=to, device_id_type=MESH)

    greet(sibling)
    for step in range(1, 8):
        greet((j, 2 * later(k, step) + c))
        greet((later(j, step), column))
        greet((later(j, step), 2 * j + c))

    @pl.when(j != k)
    def _():
        greet((j, 2 * j + c))
        pl.semaphore_wait(barrier, 23)

    @pl.when(j == k)
    def _():
        pl.semaphore_wait(barrier, 22)

    def scatter():
        out = []
        for step in range(1, 8):
            n = later(j, step)
            out.append(remote(f_hbm.at[c, n], di.at[n], root_send.at[step], di_recv.at[n], (n, column)))
        for step in range(1, 8):
            n = later(k, step)
            out.append(remote(f_hbm.at[c, n], df.at[n], root_send.at[7 + step], df_recv.at[n], (j, 2 * n + c)))
        return out

    def sinks(a, step):
        return remote(psi_hbm.at[a, j], phi.at[c, a, j], phi_send.at[a, step], phi_recv.at[a, j],
                      (k, 2 * later(k, step) + c))

    def along_column(step):
        return remote(di.at[j], di.at[j], di_send.at[step], di_recv.at[j], (later(j, step), column))

    def along_row(step):
        return remote(df.at[k], df.at[k], df_send.at[step], df_recv.at[k], (j, 2 * later(k, step) + c))

    def send_elementals(a):
        for step in range(1, 8):
            sinks(a, step).start()

        @pl.when(j != k)
        def _():
            sinks(a, 0).start()

        @pl.when(j == k)
        def _():
            pltpu.make_async_copy(psi_hbm.at[a, j], phi.at[c, a, j], phi_recv.at[a, j]).start()

    def send_pieces(buf, sems, own, along):
        wait_for(buf.at[own], sems.at[own])
        for step in range(1, 8):
            along(step).start()

    def receive(buf, sems, own):
        for step in range(1, 8):
            n = later(own, step)
            wait_for(buf.at[n], sems.at[n])

    def share(a):
        return remote(phi.at[c, a], phi.at[c, a], twin_send.at[a], twin_recv.at[a], sibling)

    def receive_elementals(a):
        for n in range(8):
            wait_for(phi.at[c, a, n], phi_recv.at[a, n])
        share(a).start()

    def receive_shared(a):
        wait_for(phi.at[twin, a], twin_recv.at[a])

    @pl.when(j == k)
    def _():
        for copy in scatter():
            copy.start()
        pltpu.make_async_copy(f_hbm.at[c, j], di.at[j], di_recv.at[j]).start()
        pltpu.make_async_copy(f_hbm.at[c, j], df.at[j], df_recv.at[j]).start()

    send_elementals(0)
    for copy in loads:
        copy.wait()
    forward_products(f, psi, g)
    back_products(f, psi, q)
    send_pieces(di, di_recv, j, along_column)
    send_elementals(1)
    from_left(f.at[0], 0, q, x)
    send_pieces(df, df_recv, k, along_row)
    from_left(f.at[1], 1, q, x)
    receive_elementals(0)
    box_products(c, 0, phi, x, p, pt)
    receive_shared(0)
    box_products(twin, 0, phi, x, p, pt)
    receive(di, di_recv, j)
    from_left(di, 0, q, r)
    from_left(di, 1, q, r)
    loop_products(0, g, r, y)
    receive_elementals(1)
    loop_products(1, g, r, y)
    box_products(c, 1, phi, x, p, pt)
    sink_transposes(c, phi, phit)
    receive(df, df_recv, k)
    sink_products(c, phi, phit, df, st, zt)
    z_copy = remote(zt.at[c], zt.at[c], z_send, z_recv, sibling)
    z_copy.start()
    receive_shared(1)
    box_products(twin, 1, phi, x, p, pt)
    sink_transposes(twin, phi, phit)
    box_traces(c, op, p, pt, out)
    box_traces(twin, op, p, pt, out)
    loop_traces(c, op, zt, phit, y, out)
    wait_for(zt.at[twin], z_recv)
    loop_traces(twin, op, zt, phit, y, out)

    for step in range(1, 8):
        for copy in (sinks(0, step), sinks(1, step), along_column(step), along_row(step)):
            copy.wait_send()
    for copy in (share(0), share(1), z_copy):
        copy.wait_send()

    @pl.when(j == k)
    def _():
        for copy in scatter():
            copy.wait_send()

    @pl.when(j != k)
    def _():
        for a in range(2):
            sinks(a, 0).wait_send()


def on_device(perambulator, elementals, op_mom):
    piece = 2 * N // 8
    anywhere = pl.BlockSpec(memory_space=pl.ANY)
    sems = pltpu.SemaphoreType.DMA
    return pl.pallas_call(
        kernel,
        out_shape=jax.ShapeDtypeStruct((2, 1, 3, 2, 4, 4), jnp.float32),
        in_specs=[pl.BlockSpec(memory_space=pltpu.SMEM), anywhere, anywhere],
        out_specs=pl.BlockSpec(memory_space=pltpu.VMEM),
        scratch_shapes=[
            pltpu.VMEM((2, 8, piece, N), BF),
            pltpu.VMEM((2, 8, piece, N), BF),
            pltpu.VMEM((2, 2, 8, piece, N), BF),
            pltpu.VMEM((8, piece, N), BF),
            pltpu.VMEM((8, piece, N), BF),
            pltpu.VMEM((2, 2, N, W), BF),
            pltpu.VMEM((2, 2, N, W), BF),
            pltpu.VMEM((2, 2, N, W), BF),
            pltpu.VMEM((2, 2, N, W), BF),
            pltpu.VMEM((2, 4, N, W), BF),
            pltpu.VMEM((2, 4, N, W), BF),
            pltpu.VMEM((2, 4, N, W), BF),
            pltpu.VMEM((2, 2, N, W), BF),
            pltpu.VMEM((2, N, W), BF),
            pltpu.VMEM((2, 4, N, W), BF),
            sems((2, 8)), sems((2, 8)), sems((8,)), sems((8,)), sems((8,)), sems((8,)), sems((16,)),
            sems((2,)), sems((2,)), sems, sems, sems((2,)),
        ],
        compiler_params=pltpu.CompilerParams(
            collective_id=0, has_side_effects=True, vmem_limit_bytes=60 * 2**20),
        cost_estimate=pl.CostEstimate(flops=20_000_000_000, bytes_accessed=4_000_000, transcendentals=0),
    )(op_mom.T, perambulator.reshape(2, 8, piece, N), elementals.reshape(2, 8, piece, N))


def solution(mesh):
    placed = (P("tsnk", "tsrc", None, None, None), P("tsrc", None, None, None, None), P())
    return jax.shard_map(
        on_device,
        mesh=mesh,
        in_specs=placed,
        out_specs=P("tsnk", "tsrc", None, None, None, None),
        check_vma=False,
    )
```

```python
import jax
import jax.numpy as jnp
from jax import lax
from jax.experimental import pallas as pl
from jax.experimental.pallas import tpu as pltpu
from jax.sharding import PartitionSpec as P

N = 384
W = 2 * N
BF = jnp.bfloat16
NN = (((1,), (0,)), ((), ()))
NT = (((1,), (1,)), ((), ()))
MESH = pl.DeviceIdType.MESH


def wait_for(ref, sem):
    pltpu.make_async_copy(ref, ref, sem).wait()


def rows(r, i):
    return jnp.concatenate([r, i], axis=1)


def block(r, i):
    return jnp.concatenate([rows(r, i), rows(-i, r)], axis=0)


def block_t(r, i):
    return jnp.concatenate([rows(r, -i), rows(i, r)], axis=0)


def mul(left, right, dims=NN):
    return lax.dot_general(left, right, dims, preferred_element_type=jnp.float32).astype(BF)


def exact(left, right):
    return lax.dot_general(
        left, right, NN, precision=lax.Precision.HIGHEST, preferred_element_type=jnp.float32)


def halves(ref):
    return ref[:, :N], ref[:, N:]


def parts(ref):
    count, depth = ref.shape[0] // 2, ref.shape[1]
    return ref[:count].reshape(count * depth, N), ref[count:].reshape(count * depth, N)


def two(ref, s):
    return jnp.concatenate([ref[s, 0], ref[s, 1]], axis=0)


def forward_products(f, psi, g):
    def body(b):
        left = jnp.concatenate([rows(*parts(f.at[s])) for s in range(2)], axis=0)
        out = mul(left, block(*parts(psi.at[b])))
        g[0, b] = out[:N]
        g[1, b] = out[N:]
    for n in range(2):
        body(n)


def back_products(f, psi, q):
    def body(s):
        left = jnp.concatenate([rows(*parts(psi.at[b])) for b in range(2)], axis=0)
        out = mul(left, block(*parts(f.at[s])), NT)
        q[s, 0] = out[:N]
        q[s, 1] = out[N:]
    for n in range(2):
        body(n)


def from_left(left, s, q, out):
    def body(b):
        out[s, b] = mul(rows(*parts(left)), block(*halves(q.at[s, b])))
    for n in range(2):
        body(n)


def loop_products(s, g, r, y):
    def body(b):
        out = mul(two(g, s), block(*halves(r.at[s, b])))
        y[s, b] = out[:N]
        y[s, 2 + b] = out[N:]
    for n in range(2):
        body(n)


def box_products(s, a, phi, x, p, pt):
    def body(b):
        out = mul(rows(*parts(phi.at[s, a])), block(*halves(x.at[s, b])))
        p[s, 2 * a + b] = out
        pt[s, 2 * a + b] = rows(out[:, :N].T, out[:, N:].T)
    for n in range(2):
        body(n)


def sink_transposes(s, phi, phit):
    def body(a):
        r, i = parts(phi.at[s, a])
        phit[s, a] = rows(r.T, i.T)
    for n in range(2):
        body(n)


def sink_products(s, phi, phit, df, st, zt, done):
    left = jnp.concatenate([rows(*parts(phi.at[s, a])) for a in range(2)], axis=0)
    out = mul(left, block(*parts(df)))
    st[0] = out[:N]
    st[1] = out[N:]

    def second(a):
        out = mul(two(phit, s), block_t(*halves(st.at[a])), NT)
        zt[s, 2 * a] = out[:N]
        zt[s, 2 * a + 1] = out[N:]
        done(a)
    for n in range(2):
        second(n)


def grouped(refs):
    out = []
    for ref in refs:
        for c in range(2):
            out.append(jnp.concatenate(
                [ref[32 * k:32 * k + 32, c * N:(c + 1) * N] for k in range(N // 32)], axis=1))
    return jnp.concatenate(out, axis=0)


def iotas(shape):
    return lax.broadcasted_iota(jnp.int32, shape, 0), lax.broadcasted_iota(jnp.int32, shape, 1)


def diagonal(left, right):
    acc = lax.dot_general(grouped(left), grouped(right), NT, preferred_element_type=jnp.float32)
    r, c = iotas(acc.shape)
    kept = jnp.where(r % 32 == c % 32, acc, 0.0)
    return jnp.sum(kept.reshape(acc.shape[0] // 32, 32, acc.shape[1]), axis=1)


def chosen(op, which, index):
    out = jnp.zeros(index.shape, jnp.int32)
    for p in range(4):
        out = jnp.where(index == p, op[which, p], out)
    return out


def as_f32(mask):
    return jnp.where(mask, 1.0, 0.0).astype(jnp.float32)


def put(out, s, k, table):
    out[s, 0, k, 0] = table[0:4, 0:4] - table[4:8, 4:8]
    out[s, 0, k, 1] = table[0:4, 4:8] + table[4:8, 0:4]


def box_traces(s, op, p, pt, out):
    acc = diagonal([p.at[s, k] for k in range(4)], [pt.at[s, k] for k in range(4)])
    r, c = iotas((16, 8))
    pick = (r // 8 == (c // 2) % 2) & ((r // 4) % 2 == c % 2) & (chosen(op, 0, r % 4) == c // 4)
    half = exact(as_f32(pick), acc)
    r, c = iotas((256, 16))
    pick = (r // 128 == c // 8) & ((r // 32) % 2 == (c // 4) % 2) & (chosen(op, 1, c % 4) == (r // 64) % 2)
    full = exact(half, as_f32(pick))
    r, c = iotas((16, 16))
    keep = (chosen(op, 0, c % 4) == r // 8) & (chosen(op, 1, r % 4) == c // 8)
    full = jnp.where(keep, full, 0.0)
    full = full[0:8] + full[8:16]
    put(out, s, 0, full[:, 0:8] + full[:, 8:16])


def loop_traces(s, op, zt, phit, y, out):
    acc = diagonal(
        [zt.at[s, k] for k in range(4)] + [phit.at[s, a] for a in range(2)], [y.at[s, k] for k in range(4)])
    acc = jnp.concatenate([acc, jnp.zeros((4, 256), jnp.float32)], axis=0)
    r, c = iotas((256, 8))
    pick = ((r // 32) % 2 == c // 4) & (chosen(op, 0, c % 4) == r // 128) & (chosen(op, 1, c % 4) == (r // 64) % 2)
    half = exact(acc, as_f32(pick))
    r, c = iotas((16, 16))
    rect = (r < 8) & (c < 8) & (c // 4 == chosen(op, 1, r % 4)) & ((c // 2) % 2 == chosen(op, 0, r % 4))
    tri = (r >= 8) & (c >= 8) & ((c - 8) // 2 == chosen(op, 0, r % 4))
    pick = (rect | tri) & ((r // 4) % 2 == c % 2)
    full = exact(as_f32(pick), half)
    put(out, s, 1, full[0:8])
    put(out, s, 2, full[8:16])


def kernel(op, f_hbm, psi_hbm, out, f, psi, phi, df, di, g, x, q, r, y, p, pt, phit, st, zt,
           phi_send, phi_recv, df_recv, di_recv, push_send, root_send,
           twin_send, twin_recv, z_send, z_recv, load_sem):
    j = lax.axis_index("tsnk")
    column = lax.axis_index("tsrc")
    k, c = column // 2, column % 2
    twin = 1 - c
    sibling = (j, 2 * k + twin)

    def later(place, step):
        return lax.rem(place + step, 8)

    def remote(src, dst, send, recv, to):
        return pltpu.make_async_remote_copy(
            src_ref=src, dst_ref=dst, send_sem=send, recv_sem=recv, device_id=to, device_id_type=MESH)

    loads = [pltpu.make_async_copy(psi_hbm, psi, load_sem.at[0]), pltpu.make_async_copy(f_hbm, f, load_sem.at[1])]
    for copy in loads:
        copy.start()

    barrier = pltpu.get_barrier_semaphore()

    def greet(to):
        pl.semaphore_signal(barrier, inc=1, device_id=to, device_id_type=MESH)

    greet(sibling)
    for step in range(1, 8):
        greet((j, 2 * later(k, step) + c))
        greet((later(j, step), column))
        greet((later(j, step), 2 * j + c))

    @pl.when(j != k)
    def _():
        greet((j, 2 * j + c))
        pl.semaphore_wait(barrier, 23)

    @pl.when(j == k)
    def _():
        pl.semaphore_wait(barrier, 22)

    def scatter():
        out = []
        for step in range(1, 8):
            n = later(j, step)
            out.append(remote(f_hbm.at[c, n], di.at[n], root_send.at[step], di_recv.at[n], (n, column)))
        for step in range(1, 8):
            n = later(k, step)
            out.append(remote(f_hbm.at[c, n], df.at[n], root_send.at[7 + step], df_recv.at[n], (j, 2 * n + c)))
        return out

    def sinks(a, step):
        return remote(psi_hbm.at[a, j], phi.at[c, a, j], phi_send.at[a, step], phi_recv.at[a, j],
                      (k, 2 * later(k, step) + c))

    def across(place, step):
        return lax.rem(place // 2 + step, 4) * 2 + lax.rem(place, 2)

    def pair(place):
        return place + 1 - 2 * lax.rem(place, 2)

    sent = []

    def push(buf, sems, slot, to):
        copy = remote(buf.at[slot], buf.at[slot], push_send.at[len(sent)], sems.at[slot], to)
        copy.start()
        sent.append(copy)

    def in_row(place):
        return (j, 2 * place + c)

    def in_column(place):
        return (place, column)

    def arrive(buf, sems, slot):
        wait_for(buf.at[slot], sems.at[slot])

    def spread(buf, sems, own, slot, where):
        arrive(buf, sems, slot)
        for step in (1, 3, 2):
            push(buf, sems, slot, where(across(own, step)))

    def spread_and_pair(buf, sems, own, where):
        spread(buf, sems, own, own, where)
        push(buf, sems, own, where(pair(own)))

    def pass_on(buf, sems, own, where):
        for step in (1, 3, 2):
            slot = across(own, step)
            arrive(buf, sems, slot)
            push(buf, sems, slot, where(pair(own)))

    def send_elementals(a):
        for step in range(1, 8):
            sinks(a, step).start()

        @pl.when(j != k)
        def _():
            sinks(a, 0).start()

        @pl.when(j == k)
        def _():
            pltpu.make_async_copy(psi_hbm.at[a, j], phi.at[c, a, j], phi_recv.at[a, j]).start()

    def hand(a):
        piece = zt.at[c, pl.ds(2 * a, 2)]
        return remote(piece, piece, z_send.at[a], z_recv.at[a], sibling)

    def share(a):
        return remote(phi.at[c, a], phi.at[c, a], twin_send.at[a], twin_recv.at[a], sibling)

    def receive_elementals(a):
        for n in range(8):
            wait_for(phi.at[c, a, n], phi_recv.at[a, n])
        share(a).start()

    def receive_shared(a):
        wait_for(phi.at[twin, a], twin_recv.at[a])

    @pl.when(j == k)
    def _():
        for copy in scatter():
            copy.start()
        pltpu.make_async_copy(f_hbm.at[c, j], di.at[j], di_recv.at[j]).start()
        pltpu.make_async_copy(f_hbm.at[c, j], df.at[j], df_recv.at[j]).start()

    send_elementals(0)
    send_elementals(1)
    for copy in loads:
        copy.wait()
    forward_products(f, psi, g)
    back_products(f, psi, q)
    from_left(f.at[0], 0, q, x)
    from_left(f.at[1], 1, q, x)
    spread_and_pair(di, di_recv, j, in_column)
    spread_and_pair(df, df_recv, k, in_row)
    receive_elementals(0)
    box_products(c, 0, phi, x, p, pt)
    receive_shared(0)
    box_products(twin, 0, phi, x, p, pt)
    spread(di, di_recv, j, pair(j), in_column)
    spread(df, df_recv, k, pair(k), in_row)
    receive_elementals(1)
    box_products(c, 1, phi, x, p, pt)
    sink_transposes(c, phi, phit)
    receive_shared(1)
    box_products(twin, 1, phi, x, p, pt)
    sink_transposes(twin, phi, phit)
    box_traces(c, op, p, pt, out)
    box_traces(twin, op, p, pt, out)
    for step in (1, 3, 2):
        arrive(di, di_recv, across(j, step))
        arrive(di, di_recv, across(pair(j), step))
    from_left(di, 0, q, r)
    from_left(di, 1, q, r)
    loop_products(0, g, r, y)
    loop_products(1, g, r, y)
    for step in (1, 3, 2):
        arrive(df, df_recv, across(k, step))
        arrive(df, df_recv, across(pair(k), step))
    sink_products(c, phi, phit, df, st, zt, lambda a: hand(a).start())
    loop_traces(c, op, zt, phit, y, out)
    for a in range(2):
        wait_for(zt.at[twin, pl.ds(2 * a, 2)], z_recv.at[a])
    loop_traces(twin, op, zt, phit, y, out)

    for step in range(1, 8):
        for copy in (sinks(0, step), sinks(1, step)):
            copy.wait_send()
    for copy in sent + [share(0), share(1), hand(0), hand(1)]:
        copy.wait_send()

    @pl.when(j == k)
    def _():
        for copy in scatter():
            copy.wait_send()

    @pl.when(j != k)
    def _():
        for a in range(2):
            sinks(a, 0).wait_send()


def on_device(perambulator, elementals, op_mom):
    piece = 2 * N // 8
    anywhere = pl.BlockSpec(memory_space=pl.ANY)
    sems = pltpu.SemaphoreType.DMA
    return pl.pallas_call(
        kernel,
        out_shape=jax.ShapeDtypeStruct((2, 1, 3, 2, 4, 4), jnp.float32),
        in_specs=[pl.BlockSpec(memory_space=pltpu.SMEM), anywhere, anywhere],
        out_specs=pl.BlockSpec(memory_space=pltpu.VMEM),
        scratch_shapes=[
            pltpu.VMEM((2, 8, piece, N), BF),
            pltpu.VMEM((2, 8, piece, N), BF),
            pltpu.VMEM((2, 2, 8, piece, N), BF),
            pltpu.VMEM((8, piece, N), BF),
            pltpu.VMEM((8, piece, N), BF),
            pltpu.VMEM((2, 2, N, W), BF),
            pltpu.VMEM((2, 2, N, W), BF),
            pltpu.VMEM((2, 2, N, W), BF),
            pltpu.VMEM((2, 2, N, W), BF),
            pltpu.VMEM((2, 4, N, W), BF),
            pltpu.VMEM((2, 4, N, W), BF),
            pltpu.VMEM((2, 4, N, W), BF),
            pltpu.VMEM((2, 2, N, W), BF),
            pltpu.VMEM((2, N, W), BF),
            pltpu.VMEM((2, 4, N, W), BF),
            sems((2, 8)), sems((2, 8)), sems((8,)), sems((8,)), sems((16,)), sems((16,)),
            sems((2,)), sems((2,)), sems((2,)), sems((2,)), sems((2,)),
        ],
        compiler_params=pltpu.CompilerParams(
            collective_id=0, has_side_effects=True, vmem_limit_bytes=60 * 2**20),
        cost_estimate=pl.CostEstimate(flops=20_000_000_000, bytes_accessed=4_000_000, transcendentals=0),
    )(op_mom.T, perambulator.reshape(2, 8, piece, N), elementals.reshape(2, 8, piece, N))


def solution(mesh):
    placed = (P("tsnk", "tsrc", None, None, None), P("tsrc", None, None, None, None), P())
    return jax.shard_map(
        on_device,
        mesh=mesh,
        in_specs=placed,
        out_specs=P("tsnk", "tsrc", None, None, None, None),
        check_vma=False,
    )
```

```python
import jax
import jax.numpy as jnp
from jax import lax
from jax.experimental import pallas as pl
from jax.experimental.pallas import tpu as pltpu
from jax.sharding import PartitionSpec as P

N = 384
W = 2 * N
BF = jnp.bfloat16
NN = (((1,), (0,)), ((), ()))
NT = (((1,), (1,)), ((), ()))
MESH = pl.DeviceIdType.MESH


def wait_for(ref, sem):
    pltpu.make_async_copy(ref, ref, sem).wait()


def rows(r, i):
    return jnp.concatenate([r, i], axis=1)


def block(r, i):
    return jnp.concatenate([rows(r, i), rows(-i, r)], axis=0)


def block_t(r, i):
    return jnp.concatenate([rows(r, -i), rows(i, r)], axis=0)


def mul(left, right, dims=NN):
    return lax.dot_general(left, right, dims, preferred_element_type=jnp.float32).astype(BF)


def exact(left, right):
    return lax.dot_general(
        left, right, NN, precision=lax.Precision.HIGHEST, preferred_element_type=jnp.float32)


def halves(ref):
    return ref[:, :N], ref[:, N:]


def parts(ref):
    count, depth = ref.shape[0] // 2, ref.shape[1]
    return ref[:count].reshape(count * depth, N), ref[count:].reshape(count * depth, N)


def two(ref, s):
    return jnp.concatenate([ref[s, 0], ref[s, 1]], axis=0)


def forward_products(f, psi, g):
    def body(b):
        left = jnp.concatenate([rows(*parts(f.at[s])) for s in range(2)], axis=0)
        out = mul(left, block(*parts(psi.at[b])))
        g[0, b] = out[:N]
        g[1, b] = out[N:]
    for n in range(2):
        body(n)


def back_products(f, psi, q):
    def body(s):
        left = jnp.concatenate([rows(*parts(psi.at[b])) for b in range(2)], axis=0)
        out = mul(left, block(*parts(f.at[s])), NT)
        q[s, 0] = out[:N]
        q[s, 1] = out[N:]
    for n in range(2):
        body(n)


def from_left(left, s, q, out):
    def body(b):
        out[s, b] = mul(rows(*parts(left)), block(*halves(q.at[s, b])))
    for n in range(2):
        body(n)


def loop_products(s, g, r, y):
    def body(b):
        out = mul(two(g, s), block(*halves(r.at[s, b])))
        y[s, b] = out[:N]
        y[s, 2 + b] = out[N:]
    for n in range(2):
        body(n)


def box_products(s, a, phi, x, p, pt):
    def body(b):
        out = mul(rows(*parts(phi.at[s, a])), block(*halves(x.at[s, b])))
        p[s, 2 * a + b] = out
        pt[s, 2 * a + b] = rows(out[:, :N].T, out[:, N:].T)
    for n in range(2):
        body(n)


def sink_transposes(s, phi, phit):
    def body(a):
        r, i = parts(phi.at[s, a])
        phit[s, a] = rows(r.T, i.T)
    for n in range(2):
        body(n)


def sink_products(s, phi, phit, df, st, zt, done):
    left = jnp.concatenate([rows(*parts(phi.at[s, a])) for a in range(2)], axis=0)
    out = mul(left, block(*parts(df)))
    st[0] = out[:N]
    st[1] = out[N:]

    def second(a):
        out = mul(two(phit, s), block_t(*halves(st.at[a])), NT)
        zt[s, 2 * a] = out[:N]
        zt[s, 2 * a + 1] = out[N:]
        done(a)
    for n in range(2):
        second(n)


def grouped(refs):
    out = []
    for ref in refs:
        for c in range(2):
            out.append(jnp.concatenate(
                [ref[32 * k:32 * k + 32, c * N:(c + 1) * N] for k in range(N // 32)], axis=1))
    return jnp.concatenate(out, axis=0)


def iotas(shape):
    return lax.broadcasted_iota(jnp.int32, shape, 0), lax.broadcasted_iota(jnp.int32, shape, 1)


def diagonal(left, right):
    acc = lax.dot_general(grouped(left), grouped(right), NT, preferred_element_type=jnp.float32)
    r, c = iotas(acc.shape)
    kept = jnp.where(r % 32 == c % 32, acc, 0.0)
    return jnp.sum(kept.reshape(acc.shape[0] // 32, 32, acc.shape[1]), axis=1)


def chosen(op, which, index):
    out = jnp.zeros(index.shape, jnp.int32)
    for p in range(4):
        out = jnp.where(index == p, op[which, p], out)
    return out


def as_f32(mask):
    return jnp.where(mask, 1.0, 0.0).astype(jnp.float32)


def put(out, s, k, table):
    out[s, 0, k, 0] = table[0:4, 0:4] - table[4:8, 4:8]
    out[s, 0, k, 1] = table[0:4, 4:8] + table[4:8, 0:4]


def box_traces(s, op, p, pt, out):
    acc = diagonal([p.at[s, k] for k in range(4)], [pt.at[s, k] for k in range(4)])
    r, c = iotas((16, 8))
    pick = (r // 8 == (c // 2) % 2) & ((r // 4) % 2 == c % 2) & (chosen(op, 0, r % 4) == c // 4)
    half = exact(as_f32(pick), acc)
    r, c = iotas((256, 16))
    pick = (r // 128 == c // 8) & ((r // 32) % 2 == (c // 4) % 2) & (chosen(op, 1, c % 4) == (r // 64) % 2)
    full = exact(half, as_f32(pick))
    r, c = iotas((16, 16))
    keep = (chosen(op, 0, c % 4) == r // 8) & (chosen(op, 1, r % 4) == c // 8)
    full = jnp.where(keep, full, 0.0)
    full = full[0:8] + full[8:16]
    put(out, s, 0, full[:, 0:8] + full[:, 8:16])


def loop_traces(s, op, zt, phit, y, out):
    acc = diagonal(
        [zt.at[s, k] for k in range(4)] + [phit.at[s, a] for a in range(2)], [y.at[s, k] for k in range(4)])
    acc = jnp.concatenate([acc, jnp.zeros((4, 256), jnp.float32)], axis=0)
    r, c = iotas((256, 8))
    pick = ((r // 32) % 2 == c // 4) & (chosen(op, 0, c % 4) == r // 128) & (chosen(op, 1, c % 4) == (r // 64) % 2)
    half = exact(acc, as_f32(pick))
    r, c = iotas((16, 16))
    rect = (r < 8) & (c < 8) & (c // 4 == chosen(op, 1, r % 4)) & ((c // 2) % 2 == chosen(op, 0, r % 4))
    tri = (r >= 8) & (c >= 8) & ((c - 8) // 2 == chosen(op, 0, r % 4))
    pick = (rect | tri) & ((r // 4) % 2 == c % 2)
    full = exact(as_f32(pick), half)
    put(out, s, 1, full[0:8])
    put(out, s, 2, full[8:16])


def kernel(op, f_hbm, psi_hbm, out, f, psi, phi, df, di, g, x, q, r, y, p, pt, phit, st, zt,
           phi_send, phi_recv, df_recv, di_recv, push_send, root_send,
           twin_send, twin_recv, z_send, z_recv, load_sem):
    j = lax.axis_index("tsnk")
    column = lax.axis_index("tsrc")
    k, c = column // 2, column % 2
    twin = 1 - c
    sibling = (j, 2 * k + twin)

    def later(place, step):
        return lax.rem(place + step, 8)

    def remote(src, dst, send, recv, to):
        return pltpu.make_async_remote_copy(
            src_ref=src, dst_ref=dst, send_sem=send, recv_sem=recv, device_id=to, device_id_type=MESH)

    loads = [pltpu.make_async_copy(psi_hbm, psi, load_sem.at[0]), pltpu.make_async_copy(f_hbm, f, load_sem.at[1])]
    for copy in loads:
        copy.start()

    barrier = pltpu.get_barrier_semaphore()

    def greet(to):
        pl.semaphore_signal(barrier, inc=1, device_id=to, device_id_type=MESH)

    greet(sibling)
    for step in range(1, 8):
        greet((j, 2 * later(k, step) + c))
        greet((later(j, step), column))
        greet((later(j, step), 2 * j + c))

    @pl.when(j != k)
    def _():
        greet((j, 2 * j + c))
        pl.semaphore_wait(barrier, 23)

    @pl.when(j == k)
    def _():
        pl.semaphore_wait(barrier, 22)

    def scatter():
        out = []
        for step in range(1, 8):
            n = later(j, step)
            out.append(remote(f_hbm.at[c, n], di.at[n], root_send.at[step], di_recv.at[n], (n, column)))
        for step in range(1, 8):
            n = later(k, step)
            out.append(remote(f_hbm.at[c, n], df.at[n], root_send.at[7 + step], df_recv.at[n], (j, 2 * n + c)))
        return out

    def sinks(a, step):
        return remote(psi_hbm.at[a, j], phi.at[c, a, j], phi_send.at[a, step], phi_recv.at[a, j],
                      (k, 2 * later(k, step) + c))

    def across(place, step):
        return lax.rem(place // 2 + step, 4) * 2 + lax.rem(place, 2)

    def pair(place):
        return place + 1 - 2 * lax.rem(place, 2)

    sent = []

    def push(buf, sems, slot, to):
        copy = remote(buf.at[slot], buf.at[slot], push_send.at[len(sent)], sems.at[slot], to)
        copy.start()
        sent.append(copy)

    def in_row(place):
        return (j, 2 * place + c)

    def in_column(place):
        return (place, column)

    def arrive(buf, sems, slot):
        wait_for(buf.at[slot], sems.at[slot])

    def spread(buf, sems, own, slot, where):
        arrive(buf, sems, slot)
        for step in (1, 3, 2):
            push(buf, sems, slot, where(across(own, step)))

    def spread_and_pair(buf, sems, own, where):
        spread(buf, sems, own, own, where)
        push(buf, sems, own, where(pair(own)))

    def pass_on(buf, sems, own, where):
        for step in (1, 3, 2):
            slot = across(own, step)
            arrive(buf, sems, slot)
            push(buf, sems, slot, where(pair(own)))

    def send_elementals(a):
        for step in range(1, 8):
            sinks(a, step).start()

        @pl.when(j != k)
        def _():
            sinks(a, 0).start()

        @pl.when(j == k)
        def _():
            pltpu.make_async_copy(psi_hbm.at[a, j], phi.at[c, a, j], phi_recv.at[a, j]).start()

    def hand(a):
        piece = zt.at[c, pl.ds(2 * a, 2)]
        return remote(piece, piece, z_send.at[a], z_recv.at[a], sibling)

    def share(a):
        return remote(phi.at[c, a], phi.at[c, a], twin_send.at[a], twin_recv.at[a], sibling)

    def receive_elementals(a):
        for n in range(8):
            wait_for(phi.at[c, a, n], phi_recv.at[a, n])
        share(a).start()

    def receive_shared(a):
        wait_for(phi.at[twin, a], twin_recv.at[a])

    @pl.when(j == k)
    def _():
        for copy in scatter():
            copy.start()
        pltpu.make_async_copy(f_hbm.at[c, j], di.at[j], di_recv.at[j]).start()
        pltpu.make_async_copy(f_hbm.at[c, j], df.at[j], df_recv.at[j]).start()

    send_elementals(0)
    send_elementals(1)
    for copy in loads:
        copy.wait()
    forward_products(f, psi, g)
    back_products(f, psi, q)
    from_left(f.at[0], 0, q, x)
    from_left(f.at[1], 1, q, x)
    spread_and_pair(di, di_recv, j, in_column)
    spread_and_pair(df, df_recv, k, in_row)
    receive_elementals(0)
    box_products(c, 0, phi, x, p, pt)
    receive_shared(0)
    box_products(twin, 0, phi, x, p, pt)
    receive_elementals(1)
    box_products(c, 1, phi, x, p, pt)
    sink_transposes(c, phi, phit)
    spread(di, di_recv, j, pair(j), in_column)
    spread(df, df_recv, k, pair(k), in_row)
    receive_shared(1)
    box_products(twin, 1, phi, x, p, pt)
    sink_transposes(twin, phi, phit)
    box_traces(c, op, p, pt, out)
    box_traces(twin, op, p, pt, out)
    for step in (1, 3, 2):
        arrive(df, df_recv, across(k, step))
        arrive(df, df_recv, across(pair(k), step))
    sink_products(c, phi, phit, df, st, zt, lambda a: hand(a).start())
    for step in (1, 3, 2):
        arrive(di, di_recv, across(j, step))
        arrive(di, di_recv, across(pair(j), step))
    from_left(di, 0, q, r)
    from_left(di, 1, q, r)
    loop_products(0, g, r, y)
    loop_products(1, g, r, y)
    loop_traces(c, op, zt, phit, y, out)
    for a in range(2):
        wait_for(zt.at[twin, pl.ds(2 * a, 2)], z_recv.at[a])
    loop_traces(twin, op, zt, phit, y, out)

    for step in range(1, 8):
        for copy in (sinks(0, step), sinks(1, step)):
            copy.wait_send()
    for copy in sent + [share(0), share(1), hand(0), hand(1)]:
        copy.wait_send()

    @pl.when(j == k)
    def _():
        for copy in scatter():
            copy.wait_send()

    @pl.when(j != k)
    def _():
        for a in range(2):
            sinks(a, 0).wait_send()


def on_device(perambulator, elementals, op_mom):
    piece = 2 * N // 8
    anywhere = pl.BlockSpec(memory_space=pl.ANY)
    sems = pltpu.SemaphoreType.DMA
    return pl.pallas_call(
        kernel,
        out_shape=jax.ShapeDtypeStruct((2, 1, 3, 2, 4, 4), jnp.float32),
        in_specs=[pl.BlockSpec(memory_space=pltpu.SMEM), anywhere, anywhere],
        out_specs=pl.BlockSpec(memory_space=pltpu.VMEM),
        scratch_shapes=[
            pltpu.VMEM((2, 8, piece, N), BF),
            pltpu.VMEM((2, 8, piece, N), BF),
            pltpu.VMEM((2, 2, 8, piece, N), BF),
            pltpu.VMEM((8, piece, N), BF),
            pltpu.VMEM((8, piece, N), BF),
            pltpu.VMEM((2, 2, N, W), BF),
            pltpu.VMEM((2, 2, N, W), BF),
            pltpu.VMEM((2, 2, N, W), BF),
            pltpu.VMEM((2, 2, N, W), BF),
            pltpu.VMEM((2, 4, N, W), BF),
            pltpu.VMEM((2, 4, N, W), BF),
            pltpu.VMEM((2, 4, N, W), BF),
            pltpu.VMEM((2, 2, N, W), BF),
            pltpu.VMEM((2, N, W), BF),
            pltpu.VMEM((2, 4, N, W), BF),
            sems((2, 8)), sems((2, 8)), sems((8,)), sems((8,)), sems((16,)), sems((16,)),
            sems((2,)), sems((2,)), sems((2,)), sems((2,)), sems((2,)),
        ],
        compiler_params=pltpu.CompilerParams(
            collective_id=0, has_side_effects=True, vmem_limit_bytes=60 * 2**20),
        cost_estimate=pl.CostEstimate(flops=20_000_000_000, bytes_accessed=4_000_000, transcendentals=0),
    )(op_mom.T, perambulator.reshape(2, 8, piece, N), elementals.reshape(2, 8, piece, N))


def solution(mesh):
    placed = (P("tsnk", "tsrc", None, None, None), P("tsrc", None, None, None, None), P())
    return jax.shard_map(
        on_device,
        mesh=mesh,
        in_specs=placed,
        out_specs=P("tsnk", "tsrc", None, None, None, None),
        check_vma=False,
    )
```

```python
import jax
import jax.numpy as jnp
from jax import lax
from jax.experimental import pallas as pl
from jax.experimental.pallas import tpu as pltpu
from jax.sharding import PartitionSpec as P

N = 384
W = 2 * N
BF = jnp.bfloat16
NN = (((1,), (0,)), ((), ()))
NT = (((1,), (1,)), ((), ()))
MESH = pl.DeviceIdType.MESH


def wait_for(ref, sem):
    pltpu.make_async_copy(ref, ref, sem).wait()


def rows(r, i):
    return jnp.concatenate([r, i], axis=1)


def block(r, i):
    return jnp.concatenate([rows(r, i), rows(-i, r)], axis=0)


def block_t(r, i):
    return jnp.concatenate([rows(r, -i), rows(i, r)], axis=0)


def mul(left, right, dims=NN):
    return lax.dot_general(left, right, dims, preferred_element_type=jnp.float32).astype(BF)


def exact(left, right):
    return lax.dot_general(
        left, right, NN, precision=lax.Precision.HIGHEST, preferred_element_type=jnp.float32)


def halves(ref):
    return ref[:, :N], ref[:, N:]


def parts(ref):
    count, depth = ref.shape[0] // 2, ref.shape[1]
    return ref[:count].reshape(count * depth, N), ref[count:].reshape(count * depth, N)


def two(ref, s):
    return jnp.concatenate([ref[s, 0], ref[s, 1]], axis=0)


def forward_products(f, psi, g):
    def body(b):
        left = jnp.concatenate([rows(*parts(f.at[s])) for s in range(2)], axis=0)
        out = mul(left, block(*parts(psi.at[b])))
        g[0, b] = out[:N]
        g[1, b] = out[N:]
    for n in range(2):
        body(n)


def back_products(f, psi, q):
    def body(s):
        left = jnp.concatenate([rows(*parts(psi.at[b])) for b in range(2)], axis=0)
        out = mul(left, block(*parts(f.at[s])), NT)
        q[s, 0] = out[:N]
        q[s, 1] = out[N:]
    for n in range(2):
        body(n)


def from_left(left, s, q, out):
    def body(b):
        out[s, b] = mul(rows(*parts(left)), block(*halves(q.at[s, b])))
    for n in range(2):
        body(n)


def loop_products(s, g, r, y):
    def body(b):
        out = mul(two(g, s), block(*halves(r.at[s, b])))
        y[s, b] = out[:N]
        y[s, 2 + b] = out[N:]
    for n in range(2):
        body(n)


def box_products(s, a, phi, x, p, pt):
    def body(b):
        out = mul(rows(*parts(phi.at[s, a])), block(*halves(x.at[s, b])))
        p[s, 2 * a + b] = out
        pt[s, 2 * a + b] = rows(out[:, :N].T, out[:, N:].T)
    for n in range(2):
        body(n)


def sink_transposes(s, phi, phit):
    def body(a):
        r, i = parts(phi.at[s, a])
        phit[s, a] = rows(r.T, i.T)
    for n in range(2):
        body(n)


def sink_products(s, phi, phit, df, st, zt, done):
    left = jnp.concatenate([rows(*parts(phi.at[s, a])) for a in range(2)], axis=0)
    out = mul(left, block(*parts(df)))
    st[0] = out[:N]
    st[1] = out[N:]

    def second(a):
        out = mul(two(phit, s), block_t(*halves(st.at[a])), NT)
        zt[s, 2 * a] = out[:N]
        zt[s, 2 * a + 1] = out[N:]
        done(a)
    for n in range(2):
        second(n)


def grouped(refs):
    out = []
    for ref in refs:
        for c in range(2):
            out.append(jnp.concatenate(
                [ref[32 * k:32 * k + 32, c * N:(c + 1) * N] for k in range(N // 32)], axis=1))
    return jnp.concatenate(out, axis=0)


def iotas(shape):
    return lax.broadcasted_iota(jnp.int32, shape, 0), lax.broadcasted_iota(jnp.int32, shape, 1)


def diagonal(left, right):
    acc = lax.dot_general(grouped(left), grouped(right), NT, preferred_element_type=jnp.float32)
    r, c = iotas(acc.shape)
    kept = jnp.where(r % 32 == c % 32, acc, 0.0)
    return jnp.sum(kept.reshape(acc.shape[0] // 32, 32, acc.shape[1]), axis=1)


def chosen(op, which, index):
    out = jnp.zeros(index.shape, jnp.int32)
    for p in range(4):
        out = jnp.where(index == p, op[which, p], out)
    return out


def as_f32(mask):
    return jnp.where(mask, 1.0, 0.0).astype(jnp.float32)


def put(out, s, k, table):
    out[s, 0, k, 0] = table[0:4, 0:4] - table[4:8, 4:8]
    out[s, 0, k, 1] = table[0:4, 4:8] + table[4:8, 0:4]


def box_traces(s, op, p, pt, out):
    acc = diagonal([p.at[s, k] for k in range(4)], [pt.at[s, k] for k in range(4)])
    r, c = iotas((16, 8))
    pick = (r // 8 == (c // 2) % 2) & ((r // 4) % 2 == c % 2) & (chosen(op, 0, r % 4) == c // 4)
    half = exact(as_f32(pick), acc)
    r, c = iotas((256, 16))
    pick = (r // 128 == c // 8) & ((r // 32) % 2 == (c // 4) % 2) & (chosen(op, 1, c % 4) == (r // 64) % 2)
    full = exact(half, as_f32(pick))
    r, c = iotas((16, 16))
    keep = (chosen(op, 0, c % 4) == r // 8) & (chosen(op, 1, r % 4) == c // 8)
    full = jnp.where(keep, full, 0.0)
    full = full[0:8] + full[8:16]
    put(out, s, 0, full[:, 0:8] + full[:, 8:16])


def loop_traces(s, op, zt, phit, y, out):
    acc = diagonal(
        [zt.at[s, k] for k in range(4)] + [phit.at[s, a] for a in range(2)], [y.at[s, k] for k in range(4)])
    acc = jnp.concatenate([acc, jnp.zeros((4, 256), jnp.float32)], axis=0)
    r, c = iotas((256, 8))
    pick = ((r // 32) % 2 == c // 4) & (chosen(op, 0, c % 4) == r // 128) & (chosen(op, 1, c % 4) == (r // 64) % 2)
    half = exact(acc, as_f32(pick))
    r, c = iotas((16, 16))
    rect = (r < 8) & (c < 8) & (c // 4 == chosen(op, 1, r % 4)) & ((c // 2) % 2 == chosen(op, 0, r % 4))
    tri = (r >= 8) & (c >= 8) & ((c - 8) // 2 == chosen(op, 0, r % 4))
    pick = (rect | tri) & ((r // 4) % 2 == c % 2)
    full = exact(as_f32(pick), half)
    put(out, s, 1, full[0:8])
    put(out, s, 2, full[8:16])


def kernel(op, f_hbm, psi_hbm, out, f, psi, phi, df, di, g, x, q, r, y, p, pt, phit, st, zt,
           phi_send, phi_recv, df_recv, di_recv, push_send, root_send,
           twin_send, twin_recv, z_send, z_recv, load_sem):
    j = lax.axis_index("tsnk")
    column = lax.axis_index("tsrc")
    k, c = column // 2, column % 2
    twin = 1 - c
    sibling = (j, 2 * k + twin)

    def later(place, step):
        return lax.rem(place + step, 8)

    def remote(src, dst, send, recv, to):
        return pltpu.make_async_remote_copy(
            src_ref=src, dst_ref=dst, send_sem=send, recv_sem=recv, device_id=to, device_id_type=MESH)

    loads = [pltpu.make_async_copy(psi_hbm, psi, load_sem.at[0]), pltpu.make_async_copy(f_hbm, f, load_sem.at[1])]
    for copy in loads:
        copy.start()

    barrier = pltpu.get_barrier_semaphore()

    def greet(to):
        pl.semaphore_signal(barrier, inc=1, device_id=to, device_id_type=MESH)

    greet(sibling)
    for step in range(1, 8):
        greet((j, 2 * later(k, step) + c))
        greet((later(j, step), column))
        greet((later(j, step), 2 * j + c))

    @pl.when(j != k)
    def _():
        greet((j, 2 * j + c))
        pl.semaphore_wait(barrier, 23)

    @pl.when(j == k)
    def _():
        pl.semaphore_wait(barrier, 22)

    def scatter():
        out = []
        for step in range(1, 8):
            n = later(j, step)
            out.append(remote(f_hbm.at[c, n], di.at[n], root_send.at[step], di_recv.at[n], (n, column)))
        for step in range(1, 8):
            n = later(k, step)
            out.append(remote(f_hbm.at[c, n], df.at[n], root_send.at[7 + step], df_recv.at[n], (j, 2 * n + c)))
        return out

    def sinks(a, step):
        return remote(psi_hbm.at[a, j], phi.at[c, a, j], phi_send.at[a, step], phi_recv.at[a, j],
                      (k, 2 * later(k, step) + c))

    def across(place, step):
        return lax.rem(place // 2 + step, 4) * 2 + lax.rem(place, 2)

    def pair(place):
        return place + 1 - 2 * lax.rem(place, 2)

    sent = []

    def push(buf, sems, slot, to):
        copy = remote(buf.at[slot], buf.at[slot], push_send.at[len(sent)], sems.at[slot], to)
        copy.start()
        sent.append(copy)

    def in_row(place):
        return (j, 2 * place + c)

    def in_column(place):
        return (place, column)

    def arrive(buf, sems, slot):
        wait_for(buf.at[slot], sems.at[slot])

    def spread(buf, sems, own, slot, where):
        arrive(buf, sems, slot)
        for step in (1, 3, 2):
            push(buf, sems, slot, where(across(own, step)))

    def spread_and_pair(buf, sems, own, where):
        spread(buf, sems, own, own, where)
        push(buf, sems, own, where(pair(own)))

    def pass_on(buf, sems, own, where):
        for step in (1, 3, 2):
            slot = across(own, step)
            arrive(buf, sems, slot)
            push(buf, sems, slot, where(pair(own)))

    def send_elementals(a):
        for step in range(1, 8):
            sinks(a, step).start()

        @pl.when(j != k)
        def _():
            sinks(a, 0).start()

        @pl.when(j == k)
        def _():
            pltpu.make_async_copy(psi_hbm.at[a, j], phi.at[c, a, j], phi_recv.at[a, j]).start()

    def hand(a):
        piece = zt.at[c, pl.ds(2 * a, 2)]
        return remote(piece, piece, z_send.at[a], z_recv.at[a], sibling)

    def share(a):
        return remote(phi.at[c, a], phi.at[c, a], twin_send.at[a], twin_recv.at[a], sibling)

    def receive_elementals(a):
        for n in range(8):
            wait_for(phi.at[c, a, n], phi_recv.at[a, n])
        share(a).start()

    def receive_shared(a):
        wait_for(phi.at[twin, a], twin_recv.at[a])

    @pl.when(j == k)
    def _():
        for copy in scatter():
            copy.start()
        pltpu.make_async_copy(f_hbm.at[c, j], di.at[j], di_recv.at[j]).start()
        pltpu.make_async_copy(f_hbm.at[c, j], df.at[j], df_recv.at[j]).start()

    send_elementals(0)
    send_elementals(1)
    for copy in loads:
        copy.wait()
    forward_products(f, psi, g)
    back_products(f, psi, q)
    from_left(f.at[0], 0, q, x)
    from_left(f.at[1], 1, q, x)
    spread_and_pair(di, di_recv, j, in_column)
    spread_and_pair(df, df_recv, k, in_row)
    receive_elementals(0)
    box_products(c, 0, phi, x, p, pt)
    receive_shared(0)
    box_products(twin, 0, phi, x, p, pt)
    receive_elementals(1)
    box_products(c, 1, phi, x, p, pt)
    sink_transposes(c, phi, phit)
    spread(df, df_recv, k, pair(k), in_row)
    spread(di, di_recv, j, pair(j), in_column)
    receive_shared(1)
    box_products(twin, 1, phi, x, p, pt)
    sink_transposes(twin, phi, phit)
    box_traces(c, op, p, pt, out)
    box_traces(twin, op, p, pt, out)
    for step in (1, 3, 2):
        arrive(df, df_recv, across(k, step))
        arrive(df, df_recv, across(pair(k), step))
    sink_products(c, phi, phit, df, st, zt, lambda a: hand(a).start())
    for step in (1, 3, 2):
        arrive(di, di_recv, across(j, step))
        arrive(di, di_recv, across(pair(j), step))
    from_left(di, 0, q, r)
    from_left(di, 1, q, r)
    loop_products(0, g, r, y)
    loop_products(1, g, r, y)
    loop_traces(c, op, zt, phit, y, out)
    for a in range(2):
        wait_for(zt.at[twin, pl.ds(2 * a, 2)], z_recv.at[a])
    loop_traces(twin, op, zt, phit, y, out)

    for step in range(1, 8):
        for copy in (sinks(0, step), sinks(1, step)):
            copy.wait_send()
    for copy in sent + [share(0), share(1), hand(0), hand(1)]:
        copy.wait_send()

    @pl.when(j == k)
    def _():
        for copy in scatter():
            copy.wait_send()

    @pl.when(j != k)
    def _():
        for a in range(2):
            sinks(a, 0).wait_send()


def on_device(perambulator, elementals, op_mom):
    piece = 2 * N // 8
    anywhere = pl.BlockSpec(memory_space=pl.ANY)
    sems = pltpu.SemaphoreType.DMA
    return pl.pallas_call(
        kernel,
        out_shape=jax.ShapeDtypeStruct((2, 1, 3, 2, 4, 4), jnp.float32),
        in_specs=[pl.BlockSpec(memory_space=pltpu.SMEM), anywhere, anywhere],
        out_specs=pl.BlockSpec(memory_space=pltpu.VMEM),
        scratch_shapes=[
            pltpu.VMEM((2, 8, piece, N), BF),
            pltpu.VMEM((2, 8, piece, N), BF),
            pltpu.VMEM((2, 2, 8, piece, N), BF),
            pltpu.VMEM((8, piece, N), BF),
            pltpu.VMEM((8, piece, N), BF),
            pltpu.VMEM((2, 2, N, W), BF),
            pltpu.VMEM((2, 2, N, W), BF),
            pltpu.VMEM((2, 2, N, W), BF),
            pltpu.VMEM((2, 2, N, W), BF),
            pltpu.VMEM((2, 4, N, W), BF),
            pltpu.VMEM((2, 4, N, W), BF),
            pltpu.VMEM((2, 4, N, W), BF),
            pltpu.VMEM((2, 2, N, W), BF),
            pltpu.VMEM((2, N, W), BF),
            pltpu.VMEM((2, 4, N, W), BF),
            sems((2, 8)), sems((2, 8)), sems((8,)), sems((8,)), sems((16,)), sems((16,)),
            sems((2,)), sems((2,)), sems((2,)), sems((2,)), sems((2,)),
        ],
        compiler_params=pltpu.CompilerParams(
            collective_id=0, has_side_effects=True, vmem_limit_bytes=60 * 2**20),
        cost_estimate=pl.CostEstimate(flops=20_000_000_000, bytes_accessed=4_000_000, transcendentals=0),
    )(op_mom.T, perambulator.reshape(2, 8, piece, N), elementals.reshape(2, 8, piece, N))


def solution(mesh):
    placed = (P("tsnk", "tsrc", None, None, None), P("tsrc", None, None, None, None), P())
    return jax.shard_map(
        on_device,
        mesh=mesh,
        in_specs=placed,
        out_specs=P("tsnk", "tsrc", None, None, None, None),
        check_vma=False,
    )
```
